32 devices in a mesh: section: 2 (over y), fsdp: 16 (over z, x, core).
Axes of the slice: x: 2, y: 2, z: 4, core: 2. Of those that a mesh axis runs over, the one named last changes fastest.
Arguments:
- images: bfloat16 [64, 197, 768], P('fsdp'), may hold values from -6 to 6
- cotangent: bfloat16 [64, 197, 768], P('fsdp'), may hold values from -6 to 6
- live_slots: int32 [64], P('fsdp'), may hold values from 0 to 1, as said below
- normgain: bfloat16 [2, 768], P('section', 'fsdp'), may hold values from 0.099609375 to 1.8984375
- normbias: bfloat16 [2, 768], P('section', 'fsdp'), may hold values from -3 to 3
- qkvweight: bfloat16 [2, 768, 2304], P('section', 'fsdp'), may hold values from -0.21875 to 0.21875
- qvbias: bfloat16 [2, 1536], P('section', 'fsdp'), may hold values from -3 to 3
- outweight: bfloat16 [2, 768, 768], P('section', 'fsdp'), may hold values from -1.75 to 1.75
- outbias: bfloat16 [2, 768], P('section', 'fsdp'), may hold values from -3 to 3
- mlpgain: bfloat16 [2, 768], P('section', 'fsdp'), may hold values from 0.099609375 to 1.8984375
- mlpbias: bfloat16 [2, 768], P('section', 'fsdp'), may hold values from -3 to 3
- upweight: bfloat16 [2, 768, 3072], P('section', 'fsdp'), may hold values from -0.21875 to 0.21875
- upbias: bfloat16 [2, 3072], P('section', 'fsdp'), may hold values from -3 to 3
- downweight: bfloat16 [2, 3072, 768], P('section', 'fsdp'), may hold values from -0.109375 to 0.109375
- downbias: bfloat16 [2, 768], P('section', 'fsdp'), may hold values from -3 to 3
Outputs:
- exits: bfloat16 [2, 64, 197, 768], P('section', 'fsdp')
- entry_grads: bfloat16 [2, 64, 197, 768], P('section', 'fsdp')
- normgain_grad: float32 [2, 768], P('section', 'fsdp')
- normbias_grad: float32 [2, 768], P('section', 'fsdp')
- qkvweight_grad: float32 [2, 768, 2304], P('section', 'fsdp')
- qvbias_grad: float32 [2, 1536], P('section', 'fsdp')
- outweight_grad: float32 [2, 768, 768], P('section', 'fsdp')
- outbias_grad: float32 [2, 768], P('section', 'fsdp')
- mlpgain_grad: float32 [2, 768], P('section', 'fsdp')
- mlpbias_grad: float32 [2, 768], P('section', 'fsdp')
- upweight_grad: float32 [2, 768, 3072], P('section', 'fsdp')
- upbias_grad: float32 [2, 3072], P('section', 'fsdp')
- downweight_grad: float32 [2, 3072, 768], P('section', 'fsdp')
- downbias_grad: float32 [2, 768], P('section', 'fsdp')
The draws below stay inside these ranges and needn't reach their ends.
Inputs may be any that keep to these rules, and one draw needn't show every extreme that they name: `live_slots`: exactly 49 of the 64 slots hold an image (1); the rest are empty (0).
All inputs are finite; a program needn't handle non-finite values.
Results may differ from the reference program's by a relative error of at most 0.014.
Values may be sent and summed in bfloat16 or wider, within the bound.
A program may use at most 256 MiB of HBM per device.

```python
import jax
import jax.numpy as jnp
from jax import lax

D = 768
HEADS = 12
HEAD = 64
FF = 3072
TOKENS = 197
SLOTS = 64
LIVE = 49


def draw_live_slots(key, part):
    key = jax.random.fold_in(key, 7)
    order = jax.random.permutation(key, SLOTS)
    return (order < LIVE).astype(jnp.int32)


def steps_of(rng, extent, pieces, least, largest):
    def one(axis_at, blocks):
        steps = jax.random.uniform(jax.random.fold_in(jax.random.fold_in(rng, 6), axis_at), (blocks,), jnp.float32, least / len(pieces), largest / len(pieces))
        return jnp.repeat(jnp.exp(steps), extent[axis_at] // blocks).reshape((-1,) + (1,) * (len(extent) - axis_at - 1))

    factor_of = one(*pieces[0])
    for cut in pieces[1:]:
        factor_of = factor_of * one(*cut)
    return factor_of


def normal_values(own_key, shape, width, reach, cuts=(), dtype=jnp.bfloat16):
    factor_of = steps_of(own_key, shape, cuts, -0.22, 0.18) if cuts else 1.0
    result = jax.random.normal(own_key, shape, jnp.float32) * width * factor_of
    return jnp.minimum(jnp.maximum(result, -reach), reach).astype(dtype)


def setup_inputs(seed: int = 0) -> dict:
    seeds = jax.random.split(jax.random.key(seed), 16)
    images = normal_values(seeds[0], (SLOTS, TOKENS, D), 1.0, 6.0, ((0, 16),))
    cotangent = normal_values(seeds[1], (SLOTS, TOKENS, D), 1.0, 6.0, ((0, 16),))
    live_slots = draw_live_slots(jax.random.fold_in(seeds[15], 71), 0)
    normgain = jnp.clip(1.0 + 0.18 * jax.random.normal(seeds[3], (2, D), jnp.float32), 0.099609375, 1.8984375).astype(jnp.bfloat16)
    normbias = normal_values(seeds[4], (2, D), 0.3, 3.0, ((0, 2), (1, 16)))
    qkvweight = normal_values(seeds[5], (2, D, 3 * D), D ** -0.5, 0.21875, ((0, 2), (1, 16)))
    qvbias = normal_values(seeds[6], (2, 2 * D), 0.5, 3.0, ((0, 2), (1, 16)))
    outweight = normal_values(seeds[7], (2, D, D), (D // 64) ** -0.5, 1.75, ((0, 2), (1, 16)))
    outbias = normal_values(seeds[8], (2, D), 0.3, 3.0, ((0, 2), (1, 16)))
    mlpgain = jnp.clip(1.0 + 0.18 * jax.random.normal(seeds[9], (2, D), jnp.float32), 0.099609375, 1.8984375).astype(jnp.bfloat16)
    mlpbias = normal_values(seeds[10], (2, D), 0.3, 3.0, ((0, 2), (1, 16)))
    upweight = normal_values(seeds[11], (2, D, FF), D ** -0.5, 0.21875, ((0, 2), (1, 16)))
    upbias = normal_values(seeds[12], (2, FF), 0.5, 3.0, ((0, 2), (1, 16)))
    downweight = normal_values(seeds[13], (2, FF, D), FF ** -0.5, 0.109375, ((0, 2), (1, 16)))
    downbias = normal_values(seeds[14], (2, D), 0.3, 3.0, ((0, 2), (1, 16)))
    return dict(images=images, cotangent=cotangent, live_slots=live_slots, normgain=normgain, normbias=normbias, qkvweight=qkvweight, qvbias=qvbias, outweight=outweight, outbias=outbias, mlpgain=mlpgain, mlpbias=mlpbias, upweight=upweight, upbias=upbias, downweight=downweight, downbias=downbias)


EPSILON = 1e-06
HIGHEST = lax.Precision.HIGHEST

@jax.custom_vjp
def low(v):
    return lax.optimization_barrier(v.astype(jnp.bfloat16)).astype(jnp.float32)

@jax.custom_vjp
def low_back(v):
    return v

def low_keep(v):
    return (low(v), None)

def low_pass(kept, grad):
    return (grad,)

def back_keep(v):
    return (v, None)

def back_low(kept, grad):
    return (low(grad),)
low.defvjp(low_keep, low_pass)
low_back.defvjp(back_keep, back_low)

def layer_norm(row_data, gain_row, shift_row):
    center = row_data - lax.optimization_barrier(jnp.mean(row_data, axis=-1, keepdims=True))
    spread = lax.optimization_barrier(jnp.mean(center * center, axis=-1, keepdims=True))
    return center * lax.rsqrt(spread + EPSILON) * gain_row + shift_row

def softmax_rows(scores):
    top_score = lax.optimization_barrier(jnp.max(scores, axis=-1, keepdims=True))
    expo = jnp.exp(scores - top_score)
    return expo / lax.optimization_barrier(jnp.sum(expo, axis=-1, keepdims=True))

def product(left_side, right_side):
    return jnp.dot(left_side, right_side, precision=HIGHEST, preferred_element_type=jnp.float32)

def block_forward(params, row_data):
    normgain, normbias, qkvweight, qvbias, outweight, outbias, mlpgain, mlpbias, upweight, upbias, downweight, downbias = params
    row_count = row_data.shape[0]
    qscale = HEAD ** (-0.5)
    normed = low(layer_norm(row_data, normgain, normbias))
    joint = product(normed, qkvweight)
    queries = low(low_back((joint[:, :D] + qvbias[:D]) * qscale))
    keys_all = low(low_back(joint[:, D:2 * D]))
    values = low(low_back(joint[:, 2 * D:] + qvbias[D:]))
    head_q = queries.reshape(row_count, HEADS, HEAD)
    head_k = keys_all.reshape(row_count, HEADS, HEAD)
    head_v = values.reshape(row_count, HEADS, HEAD)
    scores = low_back(jnp.einsum('qhd,khd->hqk', head_q, head_k, precision=HIGHEST))
    attn_low = low(softmax_rows(scores))
    mixed = jnp.einsum('hqk,khd->qhd', attn_low, head_v, precision=HIGHEST).reshape(row_count, D)
    mixed = low(low_back(mixed))
    middle = row_data + low_back(product(mixed, outweight) + outbias)
    normed_mlp = low(layer_norm(middle, mlpgain, mlpbias))
    hidden_pre = low_back(product(normed_mlp, upweight) + upbias)
    hidden = low(jax.nn.gelu(hidden_pre, approximate=False))
    return middle + low_back(product(hidden, downweight) + downbias)

def relay(first_set, second_set, image_data, handoff, live_rows):

    def first_block(one_image):
        return block_forward(first_set, one_image)

    def second_block(one_image):
        return block_forward(second_set, one_image)
    leaving = lax.map(jax.checkpoint(first_block), image_data)
    handed = low(low_back(leaving * live_rows))
    arrived = lax.map(jax.checkpoint(second_block), handed + handoff)
    return (handed, arrived * live_rows)

def reference(images, cotangent, live_slots, normgain, normbias, qkvweight, qvbias, outweight, outbias, mlpgain, mlpbias, upweight, upbias, downweight, downbias):
    stacked = (normgain, normbias, qkvweight, qvbias, outweight, outbias, mlpgain, mlpbias, upweight, upbias, downweight, downbias)
    first_set = tuple((member[0].astype(jnp.float32) for member in stacked))
    second_set = tuple((member[1].astype(jnp.float32) for member in stacked))
    image_data = images.astype(jnp.float32)
    live_rows = live_slots.astype(jnp.float32)[:, None, None]

    def wrapped(first_part, second_part, image_part, handoff):
        return relay(first_part, second_part, image_part, handoff, live_rows)
    results, pullback = jax.vjp(wrapped, first_set, second_set, image_data, jnp.zeros_like(image_data))
    grads_first, grads_second, grad_images, grad_handoff = pullback((jnp.zeros_like(results[0]), cotangent.astype(jnp.float32)))
    exits = jnp.stack([results[0], results[1]]).astype(jnp.bfloat16)
    entry_grads = jnp.stack([grad_images, grad_handoff]).astype(jnp.bfloat16)
    paired = [jnp.stack([first_grad, second_grad]) for first_grad, second_grad in zip(grads_first, grads_second)]
    return (exits, entry_grads, paired[0], paired[1], paired[2], paired[3], paired[4], paired[5], paired[6], paired[7], paired[8], paired[9], paired[10], paired[11])
```

```python
import jax
import jax.numpy as jnp
from jax import lax
from jax.experimental import pallas as pl
from jax.experimental.pallas import tpu as pltpu
from jax.sharding import PartitionSpec as P

HEADS = 12
HEAD = 64
EPSILON = 1e-06
F32 = jnp.float32
BF16 = jnp.bfloat16


def dot(left, right, left_dim=1, right_dim=0):
    dims = (((left_dim,), (right_dim,)), ((), ()))
    return lax.dot_general(left, right, dims, preferred_element_type=F32)


def head_masks():
    lane = lax.broadcasted_iota(jnp.int32, (1, 2 * HEAD), 1)
    first = (lane < HEAD).astype(F32)
    return first.astype(BF16), (1.0 - first).astype(BF16)


def attention_rows(scores, tokens):
    column = lax.broadcasted_iota(jnp.int32, scores.shape, 1)
    scores = jnp.where(column < tokens, scores, -1e30)
    expo = jnp.exp(scores - jnp.max(scores, axis=-1, keepdims=True))
    return expo * (1.0 / jnp.sum(expo, axis=-1, keepdims=True))


def attend_kernel(tokens, width, joint_ref, mixed_ref):
    masks = head_masks()
    for start in range(0, width, 2 * HEAD):
        pair = slice(start, start + 2 * HEAD)
        queries = joint_ref[:, pair]
        keys = joint_ref[:, width + start : width + start + 2 * HEAD]
        values = joint_ref[:, 2 * width + start : 2 * width + start + 2 * HEAD]
        mixed = 0.0
        for mask in masks:
            attn = attention_rows(dot(queries * mask, keys, 1, 1), tokens).astype(BF16)
            mixed = mixed + dot(attn, values * mask)
        mixed_ref[:, pair] = mixed.astype(BF16)


def attend_back_kernel(tokens, width, joint_ref, mixed_grad_ref, joint_grad_ref):
    masks = head_masks()
    for start in range(0, width, 2 * HEAD):
        pair = slice(start, start + 2 * HEAD)
        key_pair = slice(width + start, width + start + 2 * HEAD)
        value_pair = slice(2 * width + start, 2 * width + start + 2 * HEAD)
        queries = joint_ref[:, pair]
        keys = joint_ref[:, key_pair]
        values = joint_ref[:, value_pair]
        mixed_grad = mixed_grad_ref[:, pair]
        query_grad = 0.0
        keys_grad = 0.0
        values_grad = 0.0
        for mask in masks:
            head_q = queries * mask
            head_g = mixed_grad * mask
            attn = attention_rows(dot(head_q, keys, 1, 1), tokens)
            attn_grad = dot(head_g, values, 1, 1)
            values_grad = values_grad + dot(attn.astype(BF16), head_g, 0, 0)
            inner = jnp.sum(attn * attn_grad, axis=-1, keepdims=True)
            scores_grad = (attn * (attn_grad - inner)).astype(BF16)
            query_grad = query_grad + dot(scores_grad, keys * mask)
            keys_grad = keys_grad + dot(scores_grad, head_q, 0, 0)
        scaled = query_grad.astype(BF16).astype(F32) * HEAD ** (-0.5)
        joint_grad_ref[:, pair] = scaled.astype(BF16)
        joint_grad_ref[:, key_pair] = keys_grad.astype(BF16)
        joint_grad_ref[:, value_pair] = values_grad.astype(BF16)


def attend(joint, tokens):
    rows, width = joint.shape[0], joint.shape[1] // 3
    return pl.pallas_call(
        lambda *refs: attend_kernel(tokens, width, *refs),
        out_shape=jax.ShapeDtypeStruct((rows, width), BF16),
        name="attend",
        compiler_params=pltpu.CompilerParams(vmem_limit_bytes=24 * 2**20),
        cost_estimate=pl.CostEstimate(
            flops=4 * rows * rows * width * 2,
            bytes_accessed=8 * rows * width,
            transcendentals=HEADS * rows * rows,
        ),
    )(joint)


def attend_back(joint, mixed_grad, tokens):
    rows, width = mixed_grad.shape
    return pl.pallas_call(
        lambda *refs: attend_back_kernel(tokens, width, *refs),
        out_shape=jax.ShapeDtypeStruct((rows, 3 * width), BF16),
        name="attend_back",
        compiler_params=pltpu.CompilerParams(vmem_limit_bytes=24 * 2**20),
        cost_estimate=pl.CostEstimate(
            flops=10 * rows * rows * width * 2,
            bytes_accessed=14 * rows * width,
            transcendentals=HEADS * rows * rows,
        ),
    )(joint, mixed_grad)


def unit_rows(row_data):
    center = row_data - jnp.mean(row_data, axis=-1, keepdims=True)
    spread = jnp.mean(center * center, axis=-1, keepdims=True)
    inverse = lax.rsqrt(spread + EPSILON)
    return center * inverse, inverse


def norm_back(row_data, gain_row, grad):
    unit, inverse = unit_rows(row_data)
    scaled = grad * gain_row
    first = jnp.mean(scaled, axis=-1, keepdims=True)
    second = jnp.mean(scaled * unit, axis=-1, keepdims=True)
    row_grad = inverse * (scaled - first - unit * second)
    return row_grad, jnp.sum(grad * unit, axis=0), jnp.sum(grad, axis=0)


def block_forward(small, large, entering, tokens):
    normgain, normbias, qvbias, outbias, mlpgain, mlpbias, upbias, downbias = small
    qkvweight, outweight, upweight, downweight = large
    width = entering.shape[1]
    row_float = entering.astype(F32)
    normed = (unit_rows(row_float)[0] * normgain + normbias).astype(BF16)
    bias = jnp.concatenate([qvbias[:width], jnp.zeros((width,), F32), qvbias[width:]])
    scale = jnp.where(jnp.arange(3 * width) < width, HEAD ** (-0.5), 1.0)
    joint = ((dot(normed, qkvweight) + bias) * scale).astype(BF16)
    mixed = attend(joint, tokens)
    middle = row_float + dot(mixed, outweight) + outbias
    normed_mlp = (unit_rows(middle)[0] * mlpgain + mlpbias).astype(BF16)
    pre = dot(normed_mlp, upweight) + upbias
    chance = 0.5 + 0.5 * lax.erf(pre * 0.5**0.5)
    density = jnp.exp(-0.5 * pre * pre) * 0.3989422804014327
    hidden = (pre * chance).astype(BF16)
    slope = (chance + pre * density).astype(BF16)
    hidden, slope = lax.optimization_barrier((hidden, slope))
    leaving = middle + dot(hidden, downweight) + downbias
    return leaving, (entering, normed, joint, mixed, middle, normed_mlp, hidden, slope)


def block_backward(small, large, saved, arriving, tokens):
    normgain, mlpgain = small[0], small[4]
    qkvweight, outweight, upweight, downweight = large
    entering, normed, joint, mixed, middle, normed_mlp, hidden, slope = saved
    down_grad = arriving.astype(BF16)
    up_grad = (dot(down_grad, downweight, 1, 1) * slope.astype(F32)).astype(BF16)
    up_grad = lax.optimization_barrier(up_grad)
    part, grad_mlpgain, grad_mlpbias = norm_back(middle, mlpgain, dot(up_grad, upweight, 1, 1))
    middle_grad = arriving + part
    out_grad = middle_grad.astype(BF16)
    mixed_grad = dot(out_grad, outweight, 1, 1).astype(BF16)
    joint_grad = attend_back(joint, mixed_grad, tokens)
    part, grad_normgain, grad_normbias = norm_back(
        entering.astype(F32), normgain, dot(joint_grad, qkvweight, 1, 1)
    )
    sums = (grad_normgain, grad_normbias, grad_mlpgain, grad_mlpbias)
    return middle_grad + part, sums, (down_grad, up_grad, out_grad, joint_grad)


def body(
    images,
    cotangent,
    live_slots,
    normgain,
    normbias,
    qkvweight,
    qvbias,
    outweight,
    outbias,
    mlpgain,
    mlpbias,
    upweight,
    upbias,
    downweight,
    downbias,
):
    section_id = lax.axis_index("section")
    peers = lax.axis_size("fsdp")
    batches, tokens, width = images.shape
    rows = -(-tokens // 16) * 16
    padding = ((0, 0), (0, rows - tokens), (0, 0))
    live = live_slots.astype(F32)

    shards = (normgain, normbias, qvbias, outbias, mlpgain, mlpbias, upbias, downbias)
    lengths = [member.shape[1] for member in shards]
    packed = jnp.concatenate([member[0].astype(F32) for member in shards])
    room = -(-packed.shape[0] // 1024) * 1024
    packed = jnp.pad(packed, (0, room - packed.shape[0])).reshape(room // 128, 128)
    packed = lax.all_gather(packed, "fsdp", axis=0, tiled=True).reshape(peers, room)
    small = []
    at = 0
    for length in lengths:
        small.append(packed[:, at : at + length].reshape(-1))
        at += length
    large = tuple(
        lax.all_gather(member[0], "fsdp", axis=0, tiled=True)
        for member in (qkvweight, outweight, upweight, downweight)
    )
    images = jnp.pad(images, padding)
    cotangent = jnp.pad(cotangent, padding)

    ticks = batches + 1
    incoming = jnp.zeros((rows, width), BF16)
    kept = []
    leavings = []
    for tick in range(ticks):
        here, there = min(tick, batches - 1), max(tick - 1, 0)
        entering = jnp.where(section_id == 0, images[here], incoming)
        leaving, saved = block_forward(small, large, entering, tokens)
        alive = jnp.where(section_id == 0, live[here], live[there])
        leaving_low = (leaving * alive).astype(BF16)
        kept.append(saved)
        leavings.append(leaving_low)
        if tick < batches:
            incoming = lax.ppermute(leaving_low, "section", [(0, 1)])

    incoming = jnp.zeros((rows, width), BF16)
    entries = [None] * ticks
    grads = [None] * ticks
    sums = None
    real_row = (jnp.arange(rows) < tokens)[:, None].astype(F32)
    for tick in reversed(range(ticks)):
        here, there = min(tick, batches - 1), max(tick - 1, 0)
        alive_here = live[here] if tick < batches else 0.0
        alive_there = live[there] if tick > 0 else 0.0
        alive = jnp.where(section_id == 0, alive_here, alive_there)
        own = jnp.where(section_id == 1, cotangent[there], incoming).astype(F32)
        arriving = own * (alive * real_row)
        entry, tick_sums, grads[tick] = block_backward(small, large, kept[tick], arriving, tokens)
        entries[tick] = entry.astype(BF16)
        sums = tick_sums if sums is None else tuple(a + b for a, b in zip(sums, tick_sums))
        if tick > 0:
            incoming = lax.ppermute(entries[tick], "section", [(1, 0)])

    def joined(members):
        return jnp.concatenate(members, axis=0)

    down_grad, up_grad, out_grad, joint_grad = (joined(m) for m in zip(*grads))
    _, normed, _, mixed, _, normed_mlp, hidden, _ = zip(*kept)

    def spread(left, right):
        total = dot(joined(left), right, 0, 0).astype(BF16)
        return lax.psum_scatter(total, "fsdp", scatter_dimension=0, tiled=True).astype(F32)[None]

    down_sum = spread(hidden, down_grad)
    up_sum = spread(normed_mlp, up_grad)
    out_sum = spread(mixed, out_grad)
    qkv_sum = spread(normed, joint_grad)

    def rows_sum(member):
        return jnp.sum(member.astype(F32), axis=0)

    joint_sum = rows_sum(joint_grad)
    vectors = (
        sums[0],
        sums[1],
        jnp.concatenate([joint_sum[:width], joint_sum[2 * width :]]),
        rows_sum(out_grad),
        sums[2],
        sums[3],
        rows_sum(up_grad),
        rows_sum(down_grad),
    )
    packed = jnp.concatenate([vector.reshape(peers, -1) for vector in vectors], axis=1)
    packed = jnp.pad(packed, ((0, 0), (0, room - packed.shape[1])))
    packed = packed.reshape(peers * room // 128, 128)
    packed = lax.psum_scatter(packed, "fsdp", scatter_dimension=0, tiled=True).reshape(1, room)
    outs = []
    at = 0
    for length in lengths:
        outs.append(packed[:, at : at + length])
        at += length

    def by_batch(members):
        return jnp.stack(
            [
                jnp.where(section_id == 0, members[b][:tokens], members[b + 1][:tokens])
                for b in range(batches)
            ]
        )[None]

    return (
        by_batch(leavings),
        by_batch(entries),
        outs[0],
        outs[1],
        qkv_sum,
        outs[2],
        out_sum,
        outs[3],
        outs[4],
        outs[5],
        up_sum,
        outs[6],
        down_sum,
        outs[7],
    )


def solution(mesh):
    in_specs = (
        P("fsdp", None, None),
        P("fsdp", None, None),
        P("fsdp"),
        P("section", "fsdp"),
        P("section", "fsdp"),
        P("section", "fsdp", None),
        P("section", "fsdp"),
        P("section", "fsdp", None),
        P("section", "fsdp"),
        P("section", "fsdp"),
        P("section", "fsdp"),
        P("section", "fsdp", None),
        P("section", "fsdp"),
        P("section", "fsdp", None),
        P("section", "fsdp"),
    )
    out_specs = (
        P("section", "fsdp", None, None),
        P("section", "fsdp", None, None),
        P("section", "fsdp"),
        P("section", "fsdp"),
        P("section", "fsdp", None),
        P("section", "fsdp"),
        P("section", "fsdp", None),
        P("section", "fsdp"),
        P("section", "fsdp"),
        P("section", "fsdp"),
        P("section", "fsdp", None),
        P("section", "fsdp"),
        P("section", "fsdp", None),
        P("section", "fsdp"),
    )
    return jax.shard_map(body, mesh=mesh, in_specs=in_specs, out_specs=out_specs, check_vma=False)
```

```python
import jax
import jax.numpy as jnp
from jax import lax
from jax.experimental import pallas as pl
from jax.experimental.pallas import tpu as pltpu
from jax.sharding import PartitionSpec as P

HEADS = 12
HEAD = 64
EPSILON = 1e-06
F32 = jnp.float32
BF16 = jnp.bfloat16


def dot(left, right, left_dim=1, right_dim=0):
    dims = (((left_dim,), (right_dim,)), ((), ()))
    return lax.dot_general(left, right, dims, preferred_element_type=F32)


def head_masks():
    lane = lax.broadcasted_iota(jnp.int32, (1, 2 * HEAD), 1)
    first = (lane < HEAD).astype(F32)
    return first.astype(BF16), (1.0 - first).astype(BF16)


def attention_rows(scores, tokens):
    column = lax.broadcasted_iota(jnp.int32, scores.shape, 1)
    scores = jnp.where(column < tokens, scores, -1e30)
    expo = jnp.exp(scores - jnp.max(scores, axis=-1, keepdims=True))
    return expo * (1.0 / jnp.sum(expo, axis=-1, keepdims=True))


def attend_kernel(tokens, width, joint_ref, mixed_ref):
    masks = head_masks()
    for start in range(0, width, 2 * HEAD):
        pair = slice(start, start + 2 * HEAD)
        queries = joint_ref[:, pair]
        keys = joint_ref[:, width + start : width + start + 2 * HEAD]
        values = joint_ref[:, 2 * width + start : 2 * width + start + 2 * HEAD]
        mixed = 0.0
        for mask in masks:
            attn = attention_rows(dot(queries * mask, keys, 1, 1), tokens).astype(BF16)
            mixed = mixed + dot(attn, values * mask)
        mixed_ref[:, pair] = mixed.astype(BF16)


def attend_back_kernel(tokens, width, joint_ref, mixed_grad_ref, joint_grad_ref):
    masks = head_masks()
    for start in range(0, width, 2 * HEAD):
        pair = slice(start, start + 2 * HEAD)
        key_pair = slice(width + start, width + start + 2 * HEAD)
        value_pair = slice(2 * width + start, 2 * width + start + 2 * HEAD)
        queries = joint_ref[:, pair]
        keys = joint_ref[:, key_pair]
        values = joint_ref[:, value_pair]
        mixed_grad = mixed_grad_ref[:, pair]
        query_grad = 0.0
        keys_grad = 0.0
        values_grad = 0.0
        for mask in masks:
            head_q = queries * mask
            head_g = mixed_grad * mask
            attn = attention_rows(dot(head_q, keys, 1, 1), tokens)
            attn_grad = dot(head_g, values, 1, 1)
            values_grad = values_grad + dot(attn.astype(BF16), head_g, 0, 0)
            inner = jnp.sum(attn * attn_grad, axis=-1, keepdims=True)
            scores_grad = (attn * (attn_grad - inner)).astype(BF16)
            query_grad = query_grad + dot(scores_grad, keys * mask)
            keys_grad = keys_grad + dot(scores_grad, head_q, 0, 0)
        scaled = query_grad.astype(BF16).astype(F32) * HEAD ** (-0.5)
        joint_grad_ref[:, pair] = scaled.astype(BF16)
        joint_grad_ref[:, key_pair] = keys_grad.astype(BF16)
        joint_grad_ref[:, value_pair] = values_grad.astype(BF16)


def attend(joint, tokens):
    rows, width = joint.shape[0], joint.shape[1] // 3
    return pl.pallas_call(
        lambda *refs: attend_kernel(tokens, width, *refs),
        out_shape=jax.ShapeDtypeStruct((rows, width), BF16),
        name="attend",
        compiler_params=pltpu.CompilerParams(vmem_limit_bytes=24 * 2**20),
        cost_estimate=pl.CostEstimate(
            flops=4 * rows * rows * width * 2,
            bytes_accessed=8 * rows * width,
            transcendentals=HEADS * rows * rows,
        ),
    )(joint)


def attend_back(joint, mixed_grad, tokens):
    rows, width = mixed_grad.shape
    return pl.pallas_call(
        lambda *refs: attend_back_kernel(tokens, width, *refs),
        out_shape=jax.ShapeDtypeStruct((rows, 3 * width), BF16),
        name="attend_back",
        compiler_params=pltpu.CompilerParams(vmem_limit_bytes=24 * 2**20),
        cost_estimate=pl.CostEstimate(
            flops=10 * rows * rows * width * 2,
            bytes_accessed=14 * rows * width,
            transcendentals=HEADS * rows * rows,
        ),
    )(joint, mixed_grad)


def unit_rows(row_data):
    center = row_data - jnp.mean(row_data, axis=-1, keepdims=True)
    spread = jnp.mean(center * center, axis=-1, keepdims=True)
    inverse = lax.rsqrt(spread + EPSILON)
    return center * inverse, inverse


def norm_back(row_data, gain_row, grad):
    unit, inverse = unit_rows(row_data)
    scaled = grad * gain_row
    first = jnp.mean(scaled, axis=-1, keepdims=True)
    second = jnp.mean(scaled * unit, axis=-1, keepdims=True)
    row_grad = inverse * (scaled - first - unit * second)
    return row_grad, jnp.sum(grad * unit, axis=0), jnp.sum(grad, axis=0)


def block_forward(small, large, entering, tokens):
    normgain, normbias, qvbias, outbias, mlpgain, mlpbias, upbias, downbias = small
    qkvweight, outweight, upweight, downweight = large
    width = entering.shape[1]
    row_float = entering.astype(F32)
    normed = (unit_rows(row_float)[0] * normgain + normbias).astype(BF16)
    bias = jnp.concatenate([qvbias[:width], jnp.zeros((width,), F32), qvbias[width:]])
    scale = jnp.where(jnp.arange(3 * width) < width, HEAD ** (-0.5), 1.0)
    joint = ((dot(normed, qkvweight) + bias) * scale).astype(BF16)
    mixed = attend(joint, tokens)
    middle = row_float + dot(mixed, outweight) + outbias
    normed_mlp = (unit_rows(middle)[0] * mlpgain + mlpbias).astype(BF16)
    pre = dot(normed_mlp, upweight) + upbias
    chance = 0.5 + 0.5 * lax.erf(pre * 0.5**0.5)
    density = jnp.exp(-0.5 * pre * pre) * 0.3989422804014327
    hidden = (pre * chance).astype(BF16)
    slope = (chance + pre * density).astype(BF16)
    hidden, slope = lax.optimization_barrier((hidden, slope))
    leaving = middle + dot(hidden, downweight) + downbias
    return leaving, (entering, normed, joint, mixed, middle, normed_mlp, hidden, slope)


def block_backward(small, large, saved, arriving, tokens):
    normgain, mlpgain = small[0], small[4]
    qkvweight, outweight, upweight, downweight = large
    entering, normed, joint, mixed, middle, normed_mlp, hidden, slope = saved
    down_grad = arriving.astype(BF16)
    up_grad = (dot(down_grad, downweight, 1, 1) * slope.astype(F32)).astype(BF16)
    up_grad = lax.optimization_barrier(up_grad)
    part, grad_mlpgain, grad_mlpbias = norm_back(middle, mlpgain, dot(up_grad, upweight, 1, 1))
    middle_grad = arriving + part
    out_grad = middle_grad.astype(BF16)
    mixed_grad = dot(out_grad, outweight, 1, 1).astype(BF16)
    joint_grad = attend_back(joint, mixed_grad, tokens)
    part, grad_normgain, grad_normbias = norm_back(
        entering.astype(F32), normgain, dot(joint_grad, qkvweight, 1, 1)
    )
    sums = (grad_normgain, grad_normbias, grad_mlpgain, grad_mlpbias)
    return middle_grad + part, sums, (down_grad, up_grad, out_grad, joint_grad)


def columns_cut(member, width):
    return [member[:, at : at + width] for at in range(0, member.shape[1], width)]


def body(
    images,
    cotangent,
    live_slots,
    normgain,
    normbias,
    qkvweight,
    qvbias,
    outweight,
    outbias,
    mlpgain,
    mlpbias,
    upweight,
    upbias,
    downweight,
    downbias,
):
    section_id = lax.axis_index("section")
    peers = lax.axis_size("fsdp")
    batches, tokens, width = images.shape
    rows = -(-tokens // 16) * 16
    padding = ((0, 0), (0, rows - tokens), (0, 0))
    live = live_slots.astype(F32)

    shards = (normgain, normbias, qvbias, outbias, mlpgain, mlpbias, upbias, downbias)
    lengths = [member.shape[1] for member in shards]
    joined_small = jnp.concatenate([member[0] for member in shards])
    room = -(-joined_small.shape[0] // (16 * width)) * 16
    matrices = (qkvweight, outweight, upweight, downweight)
    shapes = [member.shape[1:] for member in matrices]
    pieces = [cut for member in matrices for cut in columns_cut(member[0], width)]
    pieces.append(
        jnp.pad(joined_small, (0, room * width - joined_small.shape[0])).reshape(room, width)
    )
    gathered = lax.all_gather(jnp.concatenate(pieces, axis=0), "fsdp", axis=0)
    large = []
    at = 0
    for shape in shapes:
        cuts = []
        for _ in range(shape[1] // width):
            cuts.append(gathered[:, at : at + shape[0]].reshape(peers * shape[0], width))
            at += shape[0]
        large.append(jnp.concatenate(cuts, axis=1))
    flat = gathered[:, at:].reshape(peers, room * width).astype(F32)
    small = []
    at = 0
    for length in lengths:
        small.append(flat[:, at : at + length].reshape(-1))
        at += length
    images = jnp.pad(images, padding)
    cotangent = jnp.pad(cotangent, padding)

    ticks = batches + 1
    incoming = jnp.zeros((rows, width), BF16)
    kept = []
    leavings = []
    for tick in range(ticks):
        here, there = min(tick, batches - 1), max(tick - 1, 0)
        entering = jnp.where(section_id == 0, images[here], incoming)
        leaving, saved = block_forward(small, large, entering, tokens)
        alive = jnp.where(section_id == 0, live[here], live[there])
        leaving_low = (leaving * alive).astype(BF16)
        kept.append(saved)
        leavings.append(leaving_low)
        if tick < batches:
            incoming = lax.ppermute(leaving_low, "section", [(0, 1)])

    incoming = jnp.zeros((rows, width), BF16)
    entries = [None] * ticks
    grads = [None] * ticks
    sums = None
    real_row = (jnp.arange(rows) < tokens)[:, None].astype(F32)
    for tick in reversed(range(ticks)):
        here, there = min(tick, batches - 1), max(tick - 1, 0)
        alive_here = live[here] if tick < batches else 0.0
        alive_there = live[there] if tick > 0 else 0.0
        alive = jnp.where(section_id == 0, alive_here, alive_there)
        own = jnp.where(section_id == 1, cotangent[there], incoming).astype(F32)
        arriving = own * (alive * real_row)
        entry, tick_sums, grads[tick] = block_backward(small, large, kept[tick], arriving, tokens)
        entries[tick] = entry.astype(BF16)
        sums = tick_sums if sums is None else tuple(a + b for a, b in zip(sums, tick_sums))
        if tick > 0:
            incoming = lax.ppermute(entries[tick], "section", [(1, 0)])

    def joined(members):
        return jnp.concatenate(members, axis=0)

    down_grad, up_grad, out_grad, joint_grad = (joined(m) for m in zip(*grads))
    _, normed, _, mixed, _, normed_mlp, hidden, _ = zip(*kept)

    totals = (
        dot(joined(normed), joint_grad, 0, 0).astype(BF16),
        dot(joined(mixed), out_grad, 0, 0).astype(BF16),
        dot(joined(normed_mlp), up_grad, 0, 0).astype(BF16),
        dot(joined(hidden), down_grad, 0, 0).astype(BF16),
    )

    def rows_sum(member):
        return jnp.sum(member.astype(F32), axis=0)

    joint_sum = rows_sum(joint_grad)
    vectors = (
        sums[0],
        sums[1],
        jnp.concatenate([joint_sum[:width], joint_sum[2 * width :]]),
        rows_sum(out_grad),
        sums[2],
        sums[3],
        rows_sum(up_grad),
        rows_sum(down_grad),
    )
    packed = jnp.concatenate([vector.reshape(peers, -1) for vector in vectors], axis=1)
    packed = jnp.pad(packed.astype(BF16), ((0, 0), (0, room * width - packed.shape[1])))
    pieces = [
        cut.reshape(peers, -1, width) for total in totals for cut in columns_cut(total, width)
    ]
    pieces.append(packed.reshape(peers, room, width))
    stacked = jnp.concatenate(pieces, axis=1).reshape(-1, width)
    summed = lax.psum_scatter(stacked, "fsdp", scatter_dimension=0, tiled=True)
    wholes = []
    at = 0
    for shape in shapes:
        cuts = []
        for _ in range(shape[1] // width):
            cuts.append(summed[at : at + shape[0]])
            at += shape[0]
        wholes.append(jnp.concatenate(cuts, axis=1).astype(F32)[None])
    qkv_sum, out_sum, up_sum, down_sum = wholes
    flat = summed[at:].reshape(1, room * width).astype(F32)
    outs = []
    at = 0
    for length in lengths:
        outs.append(flat[:, at : at + length])
        at += length

    def by_batch(members):
        return jnp.stack(
            [
                jnp.where(section_id == 0, members[b][:tokens], members[b + 1][:tokens])
                for b in range(batches)
            ]
        )[None]

    return (
        by_batch(leavings),
        by_batch(entries),
        outs[0],
        outs[1],
        qkv_sum,
        outs[2],
        out_sum,
        outs[3],
        outs[4],
        outs[5],
        up_sum,
        outs[6],
        down_sum,
        outs[7],
    )


def solution(mesh):
    in_specs = (
        P("fsdp", None, None),
        P("fsdp", None, None),
        P("fsdp"),
        P("section", "fsdp"),
        P("section", "fsdp"),
        P("section", "fsdp", None),
        P("section", "fsdp"),
        P("section", "fsdp", None),
        P("section", "fsdp"),
        P("section", "fsdp"),
        P("section", "fsdp"),
        P("section", "fsdp", None),
        P("section", "fsdp"),
        P("section", "fsdp", None),
        P("section", "fsdp"),
    )
    out_specs = (
        P("section", "fsdp", None, None),
        P("section", "fsdp", None, None),
        P("section", "fsdp"),
        P("section", "fsdp"),
        P("section", "fsdp", None),
        P("section", "fsdp"),
        P("section", "fsdp", None),
        P("section", "fsdp"),
        P("section", "fsdp"),
        P("section", "fsdp"),
        P("section", "fsdp", None),
        P("section", "fsdp"),
        P("section", "fsdp", None),
        P("section", "fsdp"),
    )
    return jax.shard_map(body, mesh=mesh, in_specs=in_specs, out_specs=out_specs, check_vma=False)
```
